256 devices in a mesh: group: 32 (over z, y), tensor: 8 (over x, core).
Axes of the slice: x: 4, y: 4, z: 8, core: 2. Of those that a mesh axis runs over, the one named last changes fastest.
Arguments:
- states: bfloat16 [2048, 12, 5120], P('group', None, 'tensor'), may hold values from -6 to 6
- norm_gain: float32 [5120], replicated, may hold values from 0.5 to 1.5
- w_query: bfloat16 [5120, 3072], P(None, 'tensor'), may hold values from -0.078125 to 0.078125
- w_key: bfloat16 [5120, 1024], P(None, 'tensor'), may hold values from -0.078125 to 0.078125
- w_value: bfloat16 [5120, 1024], P(None, 'tensor'), may hold values from -0.078125 to 0.078125
- w_out: bfloat16 [3072, 5120], P('tensor'), may hold values from -0.109375 to 0.109375
- key_cache: bfloat16 [2048, 128, 1024], P('group', None, 'tensor'), may hold values from -64 to 64
- value_cache: bfloat16 [2048, 128, 1024], P('group', None, 'tensor'), may hold values from -6 to 6
- ancestor_group: int32 [2048, 1], replicated, may hold values from 0 to 31; in each aligned block of 64 rows (0 to 63, 64 to 127, ...) at most 4 rows name the same one
- ancestor_slot: int32 [2048], replicated, may hold values from 0 to 63
- lengths: int32 [2048], replicated, may hold values from 16 to 128
Outputs:
- attn_out: bfloat16 [2048, 12, 5120], P('group', None, 'tensor')
The draws below stay inside these ranges and needn't reach their ends.
Inputs may be any that keep to these rules, and one draw needn't show every extreme that they name: `ancestor_group`: the particles of one group (aligned blocks of 64) name no group more than 4 times.
All inputs are finite; a program needn't handle non-finite values.
Results may differ from the reference program's by a relative error of at most 0.022.
Values may be sent and summed in bfloat16 or wider, within the bound.
A program may use at most 128 MiB of HBM per device.

```python
import math
import jax
import jax.numpy as jnp
import numpy as np
from jax import lax

D = 5120
HEAD = 128
KV_HEADS = 8
Q_HEADS = 24
P_DEV = 64
CACHE = 128
STEPS = 12
PARTICLES = 2048
CAP = 4
N_GROUP = 32
N_TENSOR = 8


def draw_lengths(key, part):
    key = jax.random.fold_in(key, 7)
    key_values, key_where = jax.random.split(key)
    drawn = jax.random.randint(key_values, (PARTICLES,), CACHE // 8, CACHE + 1)
    where_full = jax.random.randint(key_where, (), 0, PARTICLES)
    return jnp.where(jnp.arange(PARTICLES) == where_full, CACHE, drawn).astype(jnp.int32)


def draw_key_cache(key, part):
    key = jax.random.fold_in(key, 11)
    key_base = jax.random.fold_in(key, 0)
    width_all = KV_HEADS * HEAD
    base = jnp.clip(jax.random.normal(key_base, (PARTICLES, CACHE, width_all), jnp.float32), -6.0, 6.0)
    return jnp.clip(base, -64.0, 64.0).astype(jnp.bfloat16)


def touch_ends(entries, key, low, top_value):
    extent = entries.shape
    spot = [jax.random.randint(jax.random.fold_in(key, axis), (), 0, extent[axis]) for axis in range(len(extent))]
    entries = entries.at[tuple(spot)].set(low)
    longest = extent.index(max(extent))
    spot[longest] = (spot[longest] + 1) % extent[longest]
    return entries.at[tuple(spot)].set(top_value)


def shard_levels(rng, shape, shards, least, top_value):
    gain, own = 1.0, jax.random.fold_in(rng, 6)
    for axis_at, blocks in shards:
        draws = jnp.exp(jax.random.uniform(jax.random.fold_in(own, axis_at), (blocks,), jnp.float32, least / len(shards), top_value / len(shards)))
        gain = gain * jnp.repeat(draws, shape[axis_at] // blocks).reshape([-1 if axis == axis_at else 1 for axis in range(len(shape))])
    return gain


def shared_out(stream_key, own, number, rows, number_of, top, reach, slope):
    sequence = jax.random.permutation(stream_key, number_of)
    heavy_load, common = load_shares(number_of, rows * top, reach, slope, True), load_shares(number_of, rows * top, reach, slope, False)
    places = jnp.arange(number_of)

    def named(sizes, offset_by):
        used = int((sizes > 0).sum())
        fixed = max(1, used // 4)
        moved = fixed + (places - fixed + offset_by * (used - fixed)) % max(1, number_of - fixed)
        return jnp.zeros((number_of,), jnp.int32).at[sequence[jnp.where(places < fixed, places, moved)]].set(jnp.asarray(sizes, jnp.int32))

    sizes = jnp.where(number % 4 == 0, named(heavy_load, number // 4), named(common, number - number // 4 - 1))
    mixed = jax.random.permutation(jax.random.fold_in(own, 3), number_of)
    giver, sink = mixed[0:number_of // 2 * 2:2], mixed[1:number_of // 2 * 2:2]
    room = jnp.minimum(sizes[giver] - 1, reach - sizes[sink]) // 2
    room = jnp.where((giver == sequence[0]) | (sink == sequence[0]) | (sizes[sink] == 0), 0, jnp.maximum(room, 0))
    moved = jax.random.randint(jax.random.fold_in(own, 4), (number_of // 2,), 0, 1 << 20) % (room + 1)
    sizes = sizes.at[giver].add(-moved).at[sink].add(moved)
    labels = jnp.searchsorted(jnp.cumsum(sizes), jnp.arange(rows * top), side="right").astype(jnp.int32)
    listing = labels.reshape(top, rows).T
    listing = listing[jax.random.permutation(jax.random.fold_in(own, 1), rows)]
    offset_by = jax.random.randint(jax.random.fold_in(own, 2), (rows, 1), 0, top)
    return jnp.take_along_axis(listing, (jnp.arange(top)[None, :] + offset_by) % top, axis=1)


def load_shares(amount, total, limit, slope, full):
    weights = [(1 << 20) // math.isqrt(rank ** slope) + 1 for rank in range(1, amount + 1)]
    largest = limit if full else min(limit, max(-(-total // amount), total * weights[0] // sum(weights)))
    least = 1 if total - largest >= amount - 1 else 0
    counts, surplus = [largest] + [least] * (amount - 1), total - largest - least * (amount - 1)
    while surplus > 0:
        movable = [i for i in range(1, amount) if counts[i] < largest] or [i for i in range(1, amount) if counts[i] < limit]
        mass, left = sum([weights[i] for i in movable]), surplus
        for i in movable:
            extra = min(limit - counts[i], max(1, left * weights[i] // mass), surplus)
            counts[i] = counts[i] + extra
            surplus = surplus - extra
    return np.array(counts)


def noise(stream_key, extent, width, bound, cuts=(), kind=jnp.bfloat16):
    entries = width * jax.random.normal(stream_key, extent, jnp.float32)
    if cuts:
        entries = entries * shard_levels(stream_key, extent, cuts, -0.22, 0.18)
    return jnp.clip(entries, -bound, bound).astype(kind)


def setup_inputs(seed: int = 0) -> dict:
    key_of = jax.random.split(jax.random.key(seed), 12)
    states = noise(key_of[0], (PARTICLES, STEPS, D), 1.0, 6.0, ((0, 32), (2, 8)))
    norm_gain = jnp.clip(1.0 + 0.1 * jax.random.normal(key_of[1], (D,), jnp.float32), 0.5, 1.5)
    w_query = noise(key_of[2], (D, Q_HEADS * HEAD), D ** -0.5, 0.078125, ((1, 8),))
    w_key = noise(key_of[3], (D, KV_HEADS * HEAD), D ** -0.5, 0.078125, ((1, 8),))
    w_value = noise(key_of[4], (D, KV_HEADS * HEAD), D ** -0.5, 0.078125, ((1, 8),))
    w_out = noise(key_of[5], (Q_HEADS * HEAD, D), (Q_HEADS * HEAD) ** -0.5, 0.109375, ((0, 8),))
    key_cache = draw_key_cache(jax.random.fold_in(key_of[11], 71), 0)
    value_cache = noise(key_of[7], (PARTICLES, CACHE, KV_HEADS * HEAD), 1.0, 6.0, ((0, 32), (2, 8)))
    ancestor_group_keys = jax.random.split(jax.random.fold_in(key_of[8], 1), PARTICLES // P_DEV)
    ancestor_group_turns = jax.random.permutation(jax.random.fold_in(key_of[8], 3), PARTICLES // P_DEV)
    ancestor_group = jax.vmap(lambda own, number: shared_out(jax.random.fold_in(key_of[8], 2), own, number, P_DEV, N_GROUP, 1, CAP, 2))(ancestor_group_keys, ancestor_group_turns).reshape((PARTICLES, 1))
    ancestor_slot = touch_ends(jax.random.randint(key_of[9], (PARTICLES,), 0, P_DEV), jax.random.fold_in(key_of[9], 1), 0, P_DEV - 1).astype(jnp.int32)
    lengths = draw_lengths(jax.random.fold_in(key_of[11], 71), 0)
    return {"states": states, "norm_gain": norm_gain, "w_query": w_query, "w_key": w_key, "w_value": w_value, "w_out": w_out, "key_cache": key_cache, "value_cache": value_cache, "ancestor_group": ancestor_group, "ancestor_slot": ancestor_slot, "lengths": lengths}


theta_base = 1000000.0
norm_eps = 1e-06

def rope_tables(positions, half_width):
    freq_index = jnp.arange(half_width, dtype=jnp.float32)
    inverse = theta_base ** (-2.0 * freq_index / (2 * half_width))
    angles = positions.astype(jnp.float32)[..., None] * inverse
    return (jnp.cos(angles), jnp.sin(angles))

def rotate(vectors, cos_table, sin_table):
    half_width = cos_table.shape[-1]
    front_half = vectors[..., :half_width]
    back_half = vectors[..., half_width:]
    cos_wide = cos_table[:, :, None, :]
    sin_wide = sin_table[:, :, None, :]
    return jnp.concatenate([front_half * cos_wide - back_half * sin_wide, back_half * cos_wide + front_half * sin_wide], axis=-1)

def finish_softmax(scores, values, form, item_count, step_count, q_local, head_size):
    peak = lax.optimization_barrier(jnp.max(scores, axis=-1, keepdims=True))
    weights = jnp.exp(scores - peak).astype(jnp.bfloat16)
    summed = lax.optimization_barrier(jnp.sum(weights.astype(jnp.float32), axis=-1))
    output = jnp.einsum(form, weights, values, preferred_element_type=jnp.float32)
    return (output.reshape(item_count, step_count, q_local, head_size), peak[..., 0].reshape(item_count, step_count, q_local), summed.reshape(item_count, step_count, q_local))

def cache_attention(queries, keys, values, spans, kv_local):
    item_count, step_count, q_local, head_size = queries.shape
    group_size = q_local // kv_local
    row_count = keys.shape[1]
    grouped = queries.reshape(item_count, step_count, kv_local, group_size, head_size)
    key_heads = keys.reshape(item_count, row_count, kv_local, head_size)
    value_heads = values.reshape(item_count, row_count, kv_local, head_size)
    scores = jnp.einsum('nsvgd,ncvd->nsvgc', grouped, key_heads, preferred_element_type=jnp.float32) * (1.0 / math.sqrt(head_size))
    usable = jnp.arange(row_count, dtype=jnp.int32)[None, :] < spans[:, None]
    scores = jnp.where(usable[:, None, None, None, :], scores, -jnp.inf)
    return finish_softmax(scores, value_heads, 'nsvgc,ncvd->nsvgd', item_count, step_count, q_local, head_size)

def fresh_attention(queries, keys, values, kv_local):
    item_count, step_count, q_local, head_size = queries.shape
    group_size = q_local // kv_local
    grouped = queries.reshape(item_count, step_count, kv_local, group_size, head_size)
    scores = jnp.einsum('nsvgd,ntvd->nsvgt', grouped, keys, preferred_element_type=jnp.float32) * (1.0 / math.sqrt(head_size))
    causal = jnp.arange(step_count, dtype=jnp.int32)[None, :] <= jnp.arange(step_count, dtype=jnp.int32)[:, None]
    scores = jnp.where(causal[None, :, None, None, :], scores, -jnp.inf)
    return finish_softmax(scores, values, 'nsvgt,ntvd->nsvgd', item_count, step_count, q_local, head_size)

def combine_parts(cache_parts, new_parts):
    cache_out, cache_peak, cache_total = cache_parts
    new_out, new_peak, new_total = new_parts
    peak = jnp.maximum(cache_peak, new_peak)
    cache_scale = jnp.exp(cache_peak - peak)
    new_scale = jnp.exp(new_peak - peak)
    upper = cache_out * cache_scale[..., None] + new_out * new_scale[..., None]
    lower = cache_total * cache_scale + new_total * new_scale
    return (upper / lower[..., None]).astype(jnp.bfloat16)

def reference(states, norm_gain, w_query, w_key, w_value, w_out, key_cache, value_cache, ancestor_group, ancestor_slot, lengths):
    row_count = PARTICLES * STEPS
    widened = states.astype(jnp.float32)
    scale_inv = lax.rsqrt(lax.optimization_barrier(jnp.mean(widened * widened, axis=-1, keepdims=True)) + norm_eps)
    normed = (widened * scale_inv * norm_gain).astype(jnp.bfloat16).reshape(row_count, D)
    queries = jnp.dot(normed, w_query, preferred_element_type=jnp.float32).reshape(PARTICLES, STEPS, Q_HEADS, HEAD)
    new_keys = jnp.dot(normed, w_key, preferred_element_type=jnp.float32).reshape(PARTICLES, STEPS, KV_HEADS, HEAD)
    new_values = jnp.dot(normed, w_value, preferred_element_type=jnp.float32).reshape(PARTICLES, STEPS, KV_HEADS, HEAD)
    ancestors = (ancestor_group[:, 0] * P_DEV + ancestor_slot).astype(jnp.int32)
    spans = jnp.take(lengths, ancestors).astype(jnp.int32)
    positions = spans[:, None] + jnp.arange(STEPS, dtype=jnp.int32)[None, :]
    cos_table, sin_table = rope_tables(positions, HEAD // 2)
    q_rot = rotate(queries, cos_table, sin_table).astype(jnp.bfloat16)
    k_rot = rotate(new_keys, cos_table, sin_table).astype(jnp.bfloat16)
    v_new = new_values.astype(jnp.bfloat16)
    cache_parts = cache_attention(q_rot, jnp.take(key_cache, ancestors, axis=0), jnp.take(value_cache, ancestors, axis=0), spans, KV_HEADS)
    new_parts = fresh_attention(q_rot, k_rot, v_new, KV_HEADS)
    attended = combine_parts(cache_parts, new_parts).reshape(row_count, Q_HEADS * HEAD)
    block_width = Q_HEADS * HEAD // N_TENSOR
    summed = jnp.zeros((row_count, D), jnp.float32)
    for shard_index in range(N_TENSOR):
        lower_edge = shard_index * block_width
        partial_value = jnp.dot(attended[:, lower_edge:lower_edge + block_width], w_out[lower_edge:lower_edge + block_width], preferred_element_type=jnp.float32)
        partial_value = lax.optimization_barrier(partial_value.astype(jnp.bfloat16))
        summed = summed + partial_value.astype(jnp.float32)
    return summed.astype(jnp.bfloat16).reshape(PARTICLES, STEPS, D)
```

```python
import functools
import math

import jax
import jax.numpy as jnp
import numpy as np
from jax import lax
from jax.experimental import pallas as pl
from jax.experimental.pallas import tpu as pltpu
from jax.sharding import PartitionSpec as P

MESH = pl.DeviceIdType.MESH
HEAD = 128
HEADS = 3
CHUNKS = 3
THETA = 1000000.0
EPS = 1e-06
LOW = -1e30
SCALE = 1.0 / math.sqrt(HEAD)
NT = (((1,), (1,)), ((), ()))
f32 = jnp.float32
bf16 = jnp.bfloat16


def dot(a, b):
    return jnp.dot(a, b, preferred_element_type=f32)


def kernel(
    dims,
    x_hbm, gain_ref, wq_hbm, wk_hbm, wv_hbm, wo_hbm, kc_hbm, vc_hbm,
    cos_hbm, sin_hbm, slot_row, slot_col, kidx, kspan,
    out_hbm,
    xg, w_v, wo_v, k_v, v_v, cos_v, sin_v,
    acc, ssq, qrot, kn, vn, newo, newl,
    sendq, recvq, sendo, recvo, att,
    mine, other, fromp, far, ring_far, side, ring_side, outv,
    local_sem, ag_send, ag_recv, q_send, q_recv, o_send, o_recv,
    p_send, p_recv, far_send, far_recv, side_send, side_recv, out_sem,
):
    ng, nt, steps, part, feat, cap, chunks = dims
    cs = steps // chunks
    rows = cs * part
    half = rows // 2
    hs = cs // 2
    block = cap * cs
    slots = ng * block
    blocks = feat // 128
    nx = nt // 2

    me = lax.axis_index("group")
    t = lax.axis_index("tensor")
    x, core = t // 2, t % 2
    xr, xl, xf = (x + 1) % nx, (x + nx - 1) % nx, (x + 2) % nx
    right, left, partner = xr * 2 + core, xl * 2 + core, x * 2 + 1 - core
    pending = []

    def remote(src, dst, ssem, rsem, dev):
        return pltpu.make_async_remote_copy(
            src_ref=src, dst_ref=dst, send_sem=ssem, recv_sem=rsem,
            device_id=dev, device_id_type=MESH,
        )

    def send(src, dst, ssem, rsem, dev):
        copy = remote(src, dst, ssem, rsem, {"tensor": dev})
        copy.start()
        pending.append(copy)

    def arrived(dst, rsem):
        remote(dst, dst, rsem, rsem, {"tensor": partner}).wait_recv()

    barrier = pltpu.get_barrier_semaphore()
    for dev in (right, left, partner):
        pl.semaphore_signal(barrier, inc=1, device_id={"tensor": dev}, device_id_type=MESH)

    def greet(i, carry):
        pl.semaphore_signal(
            barrier, inc=1, device_id={"group": (me + i) % ng}, device_id_type=MESH
        )
        return carry

    lax.fori_loop(1, ng, greet, 0)

    copies = [
        pltpu.make_async_copy(x_hbm, xg.at[t], local_sem.at[0]),
        pltpu.make_async_copy(cos_hbm, cos_v, local_sem.at[1]),
        pltpu.make_async_copy(sin_hbm, sin_v, local_sem.at[2]),
        pltpu.make_async_copy(kc_hbm, k_v, local_sem.at[3]),
        pltpu.make_async_copy(vc_hbm, v_v, local_sem.at[4]),
    ]
    sem = 5
    w_copies, wo_copies = [], []
    for j in range(nt):
        lo = j * feat
        for ref, at, wide in ((wq_hbm, 0, 384), (wk_hbm, 384, 128), (wv_hbm, 512, 128)):
            w_copies.append(
                pltpu.make_async_copy(
                    ref.at[pl.ds(lo, feat)],
                    w_v.at[j, :, pl.ds(at, wide)],
                    local_sem.at[sem],
                )
            )
            sem += 1
    for j in range(nt):
        wo_copies.append(
            pltpu.make_async_copy(
                wo_hbm.at[:, pl.ds(j * feat, feat)], wo_v.at[j], local_sem.at[sem]
            )
        )
        sem += 1
    for copy in copies[:1] + w_copies + copies[1:] + wo_copies:
        copy.start()
    copies[0].wait()
    pl.semaphore_wait(barrier, 3 + ng - 1)

    def piece(shard, c, lo=0, count=cs):
        return xg.at[shard, pl.ds(c * cs + lo, count)]

    def ag_start(c):
        own = piece(t, c)
        send(own, own, ag_send.at[c, 0], ag_recv.at[c, 0], right)
        send(own, own, ag_send.at[c, 1], ag_recv.at[c, 1], left)
        send(own, own, ag_send.at[c, 2], ag_recv.at[c, 2], partner)

    ag_start(0)
    for copy in w_copies:
        copy.wait()

    def fold(b, carry):
        j, i = b // blocks, b % blocks
        lane = jnp.broadcast_to(gain_ref[pl.ds(b, 1), :], (128, 128))
        tall = jnp.transpose(lane)
        at = pl.ds(pl.multiple_of(i * 128, 128), 128)
        for n in range(5):
            cols = slice(n * 128, (n + 1) * 128)
            w_v[j, at, cols] = (w_v[j, at, cols].astype(f32) * tall).astype(bf16)
        return carry

    lax.fori_loop(0, nt * blocks, fold, 0)

    def shard_dot(shard, c, first=False):
        xs = xg[shard, c * cs:(c + 1) * cs].reshape(rows, feat)
        product = dot(xs, w_v[shard])
        wide = xs.astype(f32)
        squares = wide[:, 0:128] * wide[:, 0:128]
        for i in range(1, blocks):
            part_ = wide[:, i * 128:(i + 1) * 128]
            squares = squares + part_ * part_
        if first:
            acc[...] = product
            ssq[...] = squares
        else:
            acc[...] += product
            ssq[...] += squares

    def shard_of(xi, co):
        return xi * 2 + co

    def project(c):
        shard_dot(t, c, True)
        arrived(piece(partner, c), ag_recv.at[c, 2])
        shard_dot(partner, c)
        sl, sr, sf = shard_of(xl, core), shard_of(xr, core), shard_of(xf, core)
        arrived(piece(sl, c), ag_recv.at[c, 0])
        send(piece(sl, c, 0, hs), piece(sl, c, 0, hs), ag_send.at[c, 3], ag_recv.at[c, 3], right)
        send(piece(sl, c), piece(sl, c), ag_send.at[c, 4], ag_recv.at[c, 4], partner)
        arrived(piece(sr, c), ag_recv.at[c, 1])
        send(piece(sr, c, hs, hs), piece(sr, c, hs, hs), ag_send.at[c, 5], ag_recv.at[c, 5], left)
        send(piece(sr, c), piece(sr, c), ag_send.at[c, 6], ag_recv.at[c, 6], partner)
        if c + 1 < chunks:
            ag_start(c + 1)
        shard_dot(sl, c)
        shard_dot(sr, c)
        arrived(piece(sf, c, 0, hs), ag_recv.at[c, 3])
        send(piece(sf, c, 0, hs), piece(sf, c, 0, hs), ag_send.at[c, 7], ag_recv.at[c, 7], partner)
        arrived(piece(sf, c, hs, hs), ag_recv.at[c, 5])
        send(piece(sf, c, hs, hs), piece(sf, c, hs, hs), ag_send.at[c, 8], ag_recv.at[c, 8], partner)
        shard_dot(sf, c)
        pl_, pr, pf = shard_of(xl, 1 - core), shard_of(xr, 1 - core), shard_of(xf, 1 - core)
        arrived(piece(pl_, c), ag_recv.at[c, 4])
        shard_dot(pl_, c)
        arrived(piece(pr, c), ag_recv.at[c, 6])
        shard_dot(pr, c)
        arrived(piece(pf, c, 0, hs), ag_recv.at[c, 7])
        arrived(piece(pf, c, hs, hs), ag_recv.at[c, 8])
        shard_dot(pf, c)
        if c == 0:
            copies[1].wait()
            copies[2].wait()
        mean = jnp.sum(ssq[...], axis=1, keepdims=True) * (1.0 / (nt * feat))
        inv = lax.rsqrt(mean + EPS)
        here = slice(c * rows, (c + 1) * rows)
        cos, sin = cos_v[here], sin_v[here]

        def turn(v):
            v = v * inv
            return (v * cos + pltpu.roll(v, 64, 1) * sin).astype(bf16)

        for h in range(HEADS):
            qrot[c, :, h * 128:(h + 1) * 128] = turn(acc[:, h * 128:(h + 1) * 128])
        kn[here] = turn(acc[:, 384:512])
        vn[here] = (acc[:, 512:640] * inv).astype(bf16)

    def route(c):
        pick = lax.broadcasted_iota(jnp.int32, (slots, rows), 0) == slot_row[...]
        pick = pick.astype(f32).astype(bf16)
        moved = dot(pick, qrot[c]).astype(bf16)
        sendq[c] = moved.reshape(ng, block, 384)

        def go(i, carry):
            g = (me + i) % ng
            remote(
                sendq.at[c, g], recvq.at[c, me], q_send.at[c], q_recv.at[c, me], {"group": g}
            ).start()
            return carry

        lax.fori_loop(1, ng, go, 0)
        recvq[c, me] = sendq[c, me]

    def fresh(c):
        keys = (c + 1) * rows
        row = lax.broadcasted_iota(jnp.int32, (rows, keys), 0)
        col = lax.broadcasted_iota(jnp.int32, (rows, keys), 1)
        same = (row % part) == (col % part)
        causal = (col // part) <= (row // part + c * cs)
        ok = same & causal
        for h in range(HEADS):
            lanes = slice(h * 128, (h + 1) * 128)
            s = lax.dot_general(qrot[c, :, lanes], kn[0:keys], NT, preferred_element_type=f32)
            s = jnp.where(ok, s * SCALE, LOW)
            m = jnp.max(s, axis=1, keepdims=True)
            w = jnp.exp(s - m).astype(bf16)
            total = jnp.sum(w.astype(f32), axis=1, keepdims=True)
            o = dot(w, vn[0:keys])
            newo[c, :, lanes] = o / total
            newl[c, h] = jnp.broadcast_to(m + jnp.log(total), (rows, 128))

    lane3 = lax.broadcasted_iota(jnp.int32, (HEADS * block, 128), 1)
    rank3 = (lax.broadcasted_iota(jnp.int32, (HEADS * block, 128), 0) % block) // cs

    def cached(c, src):
        got = recvq[c, src]
        q = jnp.concatenate([got[:, h * 128:(h + 1) * 128] for h in range(HEADS)], axis=0)
        s = None
        slot = [kidx[src * cap + r] for r in range(cap)]
        for r in range(cap):
            one = lax.dot_general(q, k_v[slot[r]], NT, preferred_element_type=f32)
            one = jnp.where(lane3 < kspan[src * cap + r], one * SCALE, LOW)
            s = one if s is None else jnp.where(rank3 == r, one, s)
        m = jnp.max(s, axis=1, keepdims=True)
        w = jnp.exp(s - m).astype(bf16).astype(f32)
        total = jnp.sum(w, axis=1, keepdims=True)
        o = None
        for r in range(cap):
            one = dot(jnp.where(rank3 == r, w, 0.0).astype(bf16), v_v[slot[r]])
            o = one if o is None else o + one
        o = (o / total).astype(bf16)
        lse = jnp.broadcast_to(m + jnp.log(total), (HEADS * block, 128))
        hi = lse.astype(bf16).astype(f32)
        mid = (lse - hi).astype(bf16).astype(f32)
        lo = (lse - hi - mid).astype(bf16).astype(f32)
        kind = lane3 % 4
        terms = jnp.where(kind == 0, hi, jnp.where(kind == 1, mid, jnp.where(kind == 2, lo, 0.0)))
        head_lane = lane3[0:block] // 4
        stat = jnp.zeros((block, 128), f32)
        for h in range(HEADS):
            stat = jnp.where(head_lane == h, terms[h * block:(h + 1) * block], stat)
        both = [o[h * block:(h + 1) * block] for h in range(HEADS)] + [stat.astype(bf16)]
        return jnp.concatenate(both, axis=1)

    def serve(c):
        recvo[c, me] = cached(c, me)

        def go(i, carry):
            src = (me + ng - i) % ng
            remote(
                recvq.at[c, src], recvq.at[c, src], q_send.at[c], q_recv.at[c, src],
                {"group": src},
            ).wait_recv()
            sendo[c, src] = cached(c, src)
            remote(
                sendo.at[c, src], recvo.at[c, me], o_send.at[c], o_recv.at[c], {"group": src}
            ).start()
            return carry

        lax.fori_loop(1, ng, go, 0)

    def combine(c):
        span = pl.ds(0, ng - 1)
        remote(
            sendo.at[c, span], recvo.at[c, span], o_send.at[c], o_recv.at[c],
            {"group": (me + 1) % ng},
        ).wait_recv()
        pick = lax.broadcasted_iota(jnp.int32, (rows, slots), 1) == slot_col[...]
        pick = pick.astype(f32).astype(bf16)
        back = dot(pick, recvo[c].reshape(slots, 512))
        lane = lax.broadcasted_iota(jnp.int32, (rows, 128), 1) // 4
        stat = back[:, 384:512]
        for h in range(HEADS):
            lanes = slice(h * 128, (h + 1) * 128)
            cache_l = jnp.sum(jnp.where(lane == h, stat, 0.0), axis=1, keepdims=True)
            gap = newl[c, h] - cache_l
            a = 1.0 / (1.0 + jnp.exp(gap))
            b = 1.0 / (1.0 + jnp.exp(-gap))
            att[:, lanes] = (back[:, lanes] * a + newo[c, :, lanes] * b).astype(bf16)

    order = (xf, xr, xl, x)

    def give(c):
        for n, xi in enumerate(order):
            other[c, n] = dot(att[...], wo_v[shard_of(xi, 1 - core)]).astype(bf16)
            send(other.at[c, n], fromp.at[c, n], p_send.at[c, n], p_recv.at[c, n], partner)
        for n, xi in enumerate(order):
            mine[c, n] = dot(att[...], wo_v[shard_of(xi, core)]).astype(bf16)

    top, low = slice(0, half), slice(half, rows)

    def chip_sum(c, n, at):
        return mine[c, n, at].astype(f32) + fromp[c, n, at].astype(f32)

    def spread(c):
        arrived(fromp.at[c, 0], p_recv.at[c, 0])
        far[c] = chip_sum(c, 0, slice(0, rows)).astype(bf16)
        send(far.at[c, pl.ds(0, half)], ring_far.at[c, 0], far_send.at[c, 0], far_recv.at[c, 0], right)
        send(far.at[c, pl.ds(half, half)], ring_far.at[c, 1], far_send.at[c, 1], far_recv.at[c, 1], left)
        arrived(fromp.at[c, 1], p_recv.at[c, 1])
        side[c, 0, 1] = chip_sum(c, 1, low).astype(bf16)
        send(side.at[c, 0, 1], ring_side.at[c, 0, 1], side_send.at[c, 0, 1], side_recv.at[c, 0, 1], right)
        arrived(fromp.at[c, 2], p_recv.at[c, 2])
        side[c, 1, 0] = chip_sum(c, 2, top).astype(bf16)
        send(side.at[c, 1, 0], ring_side.at[c, 1, 0], side_send.at[c, 1, 0], side_recv.at[c, 1, 0], left)

    def relay(c):
        arrived(ring_far.at[c, 0], far_recv.at[c, 0])
        side[c, 0, 0] = (chip_sum(c, 1, top) + ring_far[c, 0].astype(f32)).astype(bf16)
        send(side.at[c, 0, 0], ring_side.at[c, 0, 0], side_send.at[c, 0, 0], side_recv.at[c, 0, 0], right)
        arrived(ring_far.at[c, 1], far_recv.at[c, 1])
        side[c, 1, 1] = (chip_sum(c, 2, low) + ring_far[c, 1].astype(f32)).astype(bf16)
        send(side.at[c, 1, 1], ring_side.at[c, 1, 1], side_send.at[c, 1, 1], side_recv.at[c, 1, 1], left)

    outs = []

    def finish(c):
        arrived(fromp.at[c, 3], p_recv.at[c, 3])
        for n in (1, 0):
            for s in (1, 0) if n == 0 else (0, 1):
                arrived(ring_side.at[c, s, n], side_recv.at[c, s, n])
            at = slice(n * half, (n + 1) * half)
            total = chip_sum(c, 3, at)
            total = total + ring_side[c, 0, n].astype(f32) + ring_side[c, 1, n].astype(f32)
            outv[c * cs + n * hs:c * cs + (n + 1) * hs] = total.astype(bf16).reshape(hs, part, feat)
        copy = pltpu.make_async_copy(
            outv.at[pl.ds(c * cs, cs)], out_hbm.at[pl.ds(c * cs, cs)], out_sem.at[c]
        )
        copy.start()
        outs.append(copy)

    for c in range(chunks):
        project(c)
        route(c)
        fresh(c)
        if c == 0:
            copies[3].wait()
            copies[4].wait()
        if c >= 1:
            serve(c - 1)
        if c >= 2:
            combine(c - 2)
            if c == 2:
                for copy in wo_copies:
                    copy.wait()
            give(c - 2)
            spread(c - 2)
    last = chunks - 1
    if chunks < 3:
        for copy in wo_copies:
            copy.wait()
    serve(last)
    if chunks >= 3:
        relay(last - 2)
    if chunks >= 2:
        combine(last - 1)
        give(last - 1)
        spread(last - 1)
    if chunks >= 3:
        finish(last - 2)
    if chunks >= 2:
        relay(last - 1)
    combine(last)
    give(last)
    spread(last)
    if chunks >= 2:
        finish(last - 1)
    relay(last)
    finish(last)

    for copy in pending:
        copy.wait_send()
    span = pl.ds(0, ng - 1)
    for c in range(chunks):
        remote(
            sendq.at[c, span], recvq.at[c, span], q_send.at[c], q_recv.at[c, 0],
            {"group": (me + 1) % ng},
        ).wait_send()
        remote(
            sendo.at[c, span], recvo.at[c, span], o_send.at[c], o_recv.at[c],
            {"group": (me + 1) % ng},
        ).wait_send()
    for copy in outs:
        copy.wait()


def call(dims, *args):
    ng, nt, steps, part, feat, cap, chunks = dims
    cs = steps // chunks
    rows = cs * part
    block = cap * cs
    any_ = pl.BlockSpec(memory_space=pl.ANY)
    vmem = pl.BlockSpec(memory_space=pltpu.VMEM)
    smem = pl.BlockSpec(memory_space=pltpu.SMEM)
    dma = pltpu.SemaphoreType.DMA
    V = pltpu.VMEM
    scratch = [
        V((nt, steps, part, feat), bf16), V((nt, feat, 640), bf16), V((nt, 384, feat), bf16),
        V((part, 128, 128), bf16), V((part, 128, 128), bf16),
        V((steps * part, 128), f32), V((steps * part, 128), f32),
        V((rows, 640), f32), V((rows, 128), f32), V((chunks, rows, 384), bf16),
        V((steps * part, 128), bf16), V((steps * part, 128), bf16),
        V((chunks, rows, 384), f32), V((chunks, HEADS, rows, 128), f32),
        V((chunks, ng, block, 384), bf16), V((chunks, ng, block, 384), bf16),
        V((chunks, ng, block, 512), bf16), V((chunks, ng, block, 512), bf16),
        V((rows, 384), bf16),
        V((chunks, 4, rows, feat), bf16), V((chunks, 4, rows, feat), bf16),
        V((chunks, 4, rows, feat), bf16),
        V((chunks, rows, feat), bf16), V((chunks, 2, rows // 2, feat), bf16),
        V((chunks, 2, 2, rows // 2, feat), bf16), V((chunks, 2, 2, rows // 2, feat), bf16),
        V((steps, part, feat), bf16),
        dma((5 + 4 * nt,)), dma((chunks, 9)), dma((chunks, 9)),
        dma((chunks,)), dma((chunks, ng)), dma((chunks,)), dma((chunks,)),
        dma((chunks, 4)), dma((chunks, 4)), dma((chunks, 2)), dma((chunks, 2)),
        dma((chunks, 2, 2)), dma((chunks, 2, 2)), dma((chunks,)),
    ]
    return pl.pallas_call(
        functools.partial(kernel, dims),
        out_shape=jax.ShapeDtypeStruct((steps, part, feat), bf16),
        in_specs=[any_, vmem] + [any_] * 8 + [vmem, vmem, smem, smem],
        out_specs=any_,
        scratch_shapes=scratch,
        compiler_params=pltpu.CompilerParams(
            collective_id=0, has_side_effects=True, vmem_limit_bytes=62 * 1024 * 1024
        ),
    )(*args)


def local(
    states, norm_gain, w_query, w_key, w_value, w_out, key_cache, value_cache,
    ancestor_group, ancestor_slot, lengths,
):
    part, steps, feat = states.shape
    ng, nt = lax.axis_size("group"), lax.axis_size("tensor")
    cap = max(2, (2 * part + ng - 1) // ng)
    dims = (ng, nt, steps, part, feat, cap, CHUNKS)
    cs = steps // CHUNKS
    me = lax.axis_index("group")

    sources = ancestor_group[:, 0].reshape(ng, part)
    places = ancestor_slot.reshape(ng, part)
    spans = lengths.reshape(ng, part)
    asked = sources == me
    rank = jnp.cumsum(asked.astype(jnp.int32), axis=1) - 1
    chosen = asked[:, None, :] & (rank[:, None, :] == jnp.arange(cap)[None, :, None])
    kidx = jnp.sum(jnp.where(chosen, places[:, None, :], 0), axis=2).reshape(-1)
    my_lengths = lax.dynamic_index_in_dim(spans, me, 0, keepdims=False)
    own_place = (kidx[:, None] == jnp.arange(part)[None, :])
    kspan = jnp.sum(jnp.where(own_place, my_lengths[None, :], 0), axis=1)
    mine = lax.dynamic_index_in_dim(sources, me, 0, keepdims=False)
    my_place = lax.dynamic_index_in_dim(places, me, 0, keepdims=False)
    earlier = jnp.arange(part)[None, :] < jnp.arange(part)[:, None]
    my_rank = jnp.sum((mine[:, None] == mine[None, :]) & earlier, axis=1)
    slot = mine * cap + my_rank
    target = (slot[None, :] * cs + jnp.arange(cs, dtype=jnp.int32)[:, None]).reshape(-1)
    my_span = jnp.take(lengths, mine * part + my_place)
    position = (my_span[None, :] + jnp.arange(steps, dtype=jnp.int32)[:, None]).reshape(-1)
    index = jnp.arange(64, dtype=f32)
    inverse = THETA ** (-2.0 * index / 128)
    angles = position.astype(f32)[:, None] * inverse
    cos, sin = jnp.cos(angles), jnp.sin(angles)
    cos = jnp.concatenate([cos, cos], axis=1)
    sin = jnp.concatenate([-sin, sin], axis=1)

    out = call(
        dims,
        jnp.transpose(states, (1, 0, 2)),
        norm_gain.reshape(-1, 128),
        w_query, w_key, w_value, w_out, key_cache, value_cache,
        cos, sin,
        target[None, :], target[:, None],
        kidx.astype(jnp.int32), kspan.astype(jnp.int32),
    )
    return jnp.transpose(out, (1, 0, 2))


def solution(mesh):
    in_specs = (
        P("group", None, "tensor"),
        P(),
        P(None, "tensor"),
        P(None, "tensor"),
        P(None, "tensor"),
        P("tensor", None),
        P("group", None, "tensor"),
        P("group", None, "tensor"),
        P(),
        P(),
        P(),
    )
    out_specs = P("group", None, "tensor")
    return jax.shard_map(local, mesh=mesh, in_specs=in_specs, out_specs=out_specs, check_vma=False)
```

```python
import functools
import math

import jax
import jax.numpy as jnp
import numpy as np
from jax import lax
from jax.experimental import pallas as pl
from jax.experimental.pallas import tpu as pltpu
from jax.sharding import PartitionSpec as P

MESH = pl.DeviceIdType.MESH
HEAD = 128
HEADS = 3
CHUNKS = 3
ORDER = (
    "A0", "B0", "R0", "A1", "s0", "B1", "R1", "t0", "F0", "A2",
    "s1", "B2", "R2", "t1", "F1", "C0", "V0", "P0", "s2", "L0",
    "t2", "F2", "C1", "V1", "P1", "N0", "L1", "C2", "V2", "P2",
    "N1", "L2", "N2",
)
THETA = 1000000.0
EPS = 1e-06
LOW = -1e30
SCALE = 1.0 / math.sqrt(HEAD)
NT = (((1,), (1,)), ((), ()))
f32 = jnp.float32
bf16 = jnp.bfloat16


def dot(a, b):
    return jnp.dot(a, b, preferred_element_type=f32)


def kernel(
    dims,
    x_hbm, gain_ref, wq_hbm, wk_hbm, wv_hbm, wo_hbm, kc_hbm, vc_hbm,
    group_ref, place_ref, length_ref, lengths_s, turns_ref,
    out_hbm,
    xg, w_v, wo_v, k_v, v_v, cos_v, sin_v, slot_row, slot_col, table_v, table_s,
    acc, ssq, qrot, kn, vn, newo, newl,
    sendq, recvq, sendo, recvo, sendl, recvl, att,
    mine, other, fromp, far, ring_far, side, ring_side, outv,
    local_sem, ag_send, ag_recv, q_send, q_recv, o_send, o_recv, l_send, l_recv,
    p_send, p_recv, far_send, far_recv, side_send, side_recv, out_sem,
):
    ng, nt, steps, part, feat, cap, chunks = dims
    cs = steps // chunks
    rows = cs * part
    half = rows // 2
    hs = cs // 2
    block = cap * cs
    slots = ng * block
    blocks = feat // 128
    nx = nt // 2

    me = lax.axis_index("group")
    t = lax.axis_index("tensor")
    x, core = t // 2, t % 2
    xr, xl, xf = (x + 1) % nx, (x + nx - 1) % nx, (x + 2) % nx
    right, left, partner = xr * 2 + core, xl * 2 + core, x * 2 + 1 - core
    pending = []

    def remote(src, dst, ssem, rsem, dev):
        return pltpu.make_async_remote_copy(
            src_ref=src, dst_ref=dst, send_sem=ssem, recv_sem=rsem,
            device_id=dev, device_id_type=MESH,
        )

    def send(src, dst, ssem, rsem, dev):
        copy = remote(src, dst, ssem, rsem, {"tensor": dev})
        copy.start()
        pending.append(copy)

    def arrived(dst, rsem):
        remote(dst, dst, rsem, rsem, {"tensor": partner}).wait_recv()

    first = pltpu.make_async_copy(x_hbm, xg.at[t], local_sem.at[0])
    first.start()

    barrier = pltpu.get_barrier_semaphore()
    for dev in (right, left, partner):
        pl.semaphore_signal(barrier, inc=1, device_id={"tensor": dev}, device_id_type=MESH)

    def greet(i, carry):
        pl.semaphore_signal(
            barrier, inc=1, device_id={"group": (me + i) % ng}, device_id_type=MESH
        )
        return carry

    lax.fori_loop(1, ng, greet, 0)

    copies = [
        pltpu.make_async_copy(kc_hbm, k_v, local_sem.at[1]),
        pltpu.make_async_copy(vc_hbm, v_v, local_sem.at[2]),
    ]
    sem = 3
    w_copies, wo_copies = [], []
    for j in range(nt):
        lo = j * feat
        for ref, at, wide in ((wq_hbm, 0, 384), (wk_hbm, 384, 128), (wv_hbm, 512, 128)):
            w_copies.append(
                pltpu.make_async_copy(
                    ref.at[pl.ds(lo, feat)],
                    w_v.at[j, :, pl.ds(at, wide)],
                    local_sem.at[sem],
                )
            )
            sem += 1
    for j in range(nt):
        wo_copies.append(
            pltpu.make_async_copy(
                wo_hbm.at[:, pl.ds(j * feat, feat)], wo_v.at[j], local_sem.at[sem]
            )
        )
        sem += 1
    first.wait()
    pl.semaphore_wait(barrier, 3 + ng - 1)

    def piece(shard, c, lo=0, count=cs):
        return xg.at[shard, pl.ds(c * cs + lo, count)]

    def ag_start(c):
        own = piece(t, c)
        send(own, own, ag_send.at[c, 0], ag_recv.at[c, 0], right)
        send(own, own, ag_send.at[c, 1], ag_recv.at[c, 1], left)
        send(own, own, ag_send.at[c, 2], ag_recv.at[c, 2], partner)

    ag_start(0)
    for copy in w_copies:
        copy.start()
    for copy in w_copies:
        copy.wait()

    def fold(b, carry):
        j, i = b // blocks, b % blocks
        lane = jnp.broadcast_to(gain_ref[pl.ds(b, 1), :], (128, 128))
        tall = jnp.transpose(lane)
        at = pl.ds(pl.multiple_of(i * 128, 128), 128)
        for n in range(5):
            cols = slice(n * 128, (n + 1) * 128)
            w_v[j, at, cols] = (w_v[j, at, cols].astype(f32) * tall).astype(bf16)
        return carry

    lax.fori_loop(0, nt * blocks, fold, 0)

    def count(shape, axis):
        return lax.broadcasted_iota(jnp.int32, shape, axis)

    two = 128 // part
    lines = ng // two
    row_i, col_i = count((128, 128), 0), count((128, 128), 1)
    lane_l = count((lines, 128), 1)
    asked = jnp.where(group_ref[...] == me, 1, 0)
    within = lane_l % part
    rank = asked
    hop = 1
    while hop < part:
        rank = rank + jnp.where(within >= hop, pltpu.roll(rank, hop, 1), 0)
        hop *= 2
    table = jnp.zeros((lines, 128), jnp.int32)
    for r in range(cap):
        found = jnp.where((asked == 1) & (rank == r + 1), place_ref[...], 0)
        hop = 1
        while hop < part:
            found = found + jnp.where(within >= hop, pltpu.roll(found, hop, 1), 0)
            hop *= 2
        for n in range(two):
            to = n * cap + r
            moved = pltpu.roll(found, (to - (n + 1) * part + 1) % 128, 1)
            table = jnp.where(lane_l == to, moved, table)
    table_v[...] = table
    table_copy = pltpu.make_async_copy(table_v, table_s, local_sem.at[3 + 4 * nt])
    table_copy.start()

    def own_line(ref):
        line = ref[pl.ds(me // two, 1), :].astype(f32)
        best = line
        for n in range(1, two):
            best = jnp.where(me % two == n, pltpu.roll(line, 128 - n * part, 1), best)
        return best

    wide_group = jnp.broadcast_to(own_line(group_ref), (128, 128))
    wide_place = jnp.broadcast_to(own_line(place_ref), (128, 128))
    tall_group, tall_place = jnp.transpose(wide_group), jnp.transpose(wide_place)
    match = (wide_group == tall_group).astype(f32)
    row_rank = jnp.sum(jnp.where(row_i < col_i, match, 0.0), axis=0, keepdims=True)
    col_rank = jnp.sum(jnp.where(col_i < row_i, match, 0.0), axis=1, keepdims=True)
    row_slot = (wide_group[0:1] * cap + row_rank) * cs
    col_slot = (tall_group * cap + col_rank) * cs
    row_slot = jnp.where(count((1, 128), 1) < part, row_slot, 0.0)
    for n in range(1, two):
        row_slot = row_slot + jnp.where(
            count((1, 128), 1) // part == n, pltpu.roll(row_slot, n * part, 1), 0.0
        )
    for n in range(cs // two):
        ahead = row_slot + (count((1, 128), 1) // part + n * two).astype(f32)
        slot_row[:, n * 128:(n + 1) * 128] = ahead.astype(jnp.int32)
    for n in range(cs):
        slot_col[n * part:(n + 1) * part] = (col_slot[0:part] + n).astype(jnp.int32)
    which = (tall_group * (1.0 / two)).astype(jnp.int32)
    rest = tall_group.astype(jnp.int32) - which * two
    line_of = (which[0:part, 0:lines] == count((part, lines), 1)).astype(f32).astype(bf16)
    near = dot(line_of, length_ref[...].astype(f32).astype(bf16))
    at_lane = rest * part + tall_place.astype(jnp.int32)
    near = jnp.where(count((part, 128), 1) == at_lane[0:part], near, 0.0)
    span_col = jnp.sum(near, axis=1, keepdims=True)
    angle = span_col * turns_ref[0:1]
    cos_a, sin_a = jnp.cos(angle), jnp.sin(angle)
    for n in range(steps):
        cos_b, sin_b = turns_ref[8 + n:9 + n], turns_ref[8 + steps + n:9 + steps + n]
        cos_v[n * part:(n + 1) * part] = cos_a * cos_b - sin_a * sin_b
        sin_v[n * part:(n + 1) * part] = (sin_a * cos_b + cos_a * sin_b) * turns_ref[1:2]

    def shard_dot(shard, c, first=False):
        xs = xg[shard, c * cs:(c + 1) * cs].reshape(rows, feat)
        product = dot(xs, w_v[shard])
        wide = xs.astype(f32)
        squares = wide[:, 0:128] * wide[:, 0:128]
        for i in range(1, blocks):
            part_ = wide[:, i * 128:(i + 1) * 128]
            squares = squares + part_ * part_
        if first:
            acc[...] = product
            ssq[...] = squares
        else:
            acc[...] += product
            ssq[...] += squares

    def shard_of(xi, co):
        return xi * 2 + co

    sl, sr, sf = shard_of(xl, core), shard_of(xr, core), shard_of(xf, core)

    def project(c):
        shard_dot(t, c, True)
        arrived(piece(partner, c), ag_recv.at[c, 2])
        shard_dot(partner, c)
        arrived(piece(sl, c), ag_recv.at[c, 0])
        send(piece(sl, c, 0, hs), piece(sl, c, 0, hs), ag_send.at[c, 3], ag_recv.at[c, 3], right)
        send(piece(sl, c), piece(sl, c), ag_send.at[c, 4], ag_recv.at[c, 4], partner)
        arrived(piece(sr, c), ag_recv.at[c, 1])
        send(piece(sr, c, hs, hs), piece(sr, c, hs, hs), ag_send.at[c, 5], ag_recv.at[c, 5], left)
        send(piece(sr, c), piece(sr, c), ag_send.at[c, 6], ag_recv.at[c, 6], partner)
        if c + 1 < chunks:
            ag_start(c + 1)
        shard_dot(sl, c)
        shard_dot(sr, c)

    def project_rest(c):
        if c == 0:
            for copy in copies + wo_copies:
                copy.start()
        arrived(piece(sf, c, 0, hs), ag_recv.at[c, 3])
        send(piece(sf, c, 0, hs), piece(sf, c, 0, hs), ag_send.at[c, 7], ag_recv.at[c, 7], partner)
        arrived(piece(sf, c, hs, hs), ag_recv.at[c, 5])
        send(piece(sf, c, hs, hs), piece(sf, c, hs, hs), ag_send.at[c, 8], ag_recv.at[c, 8], partner)
        shard_dot(sf, c)
        pl_, pr, pf = shard_of(xl, 1 - core), shard_of(xr, 1 - core), shard_of(xf, 1 - core)
        arrived(piece(pl_, c), ag_recv.at[c, 4])
        shard_dot(pl_, c)
        arrived(piece(pr, c), ag_recv.at[c, 6])
        shard_dot(pr, c)
        arrived(piece(pf, c, 0, hs), ag_recv.at[c, 7])
        arrived(piece(pf, c, hs, hs), ag_recv.at[c, 8])
        shard_dot(pf, c)
        mean = jnp.sum(ssq[...], axis=1, keepdims=True) * (1.0 / (nt * feat))
        inv = lax.rsqrt(mean + EPS)
        here = slice(c * rows, (c + 1) * rows)
        cos, sin = cos_v[here], sin_v[here]

        def turn(v):
            v = v * inv
            return (v * cos + pltpu.roll(v, 64, 1) * sin).astype(bf16)

        for h in range(HEADS):
            qrot[c, :, h * 128:(h + 1) * 128] = turn(acc[:, h * 128:(h + 1) * 128])
        kn[here] = turn(acc[:, 384:512])
        vn[here] = (acc[:, 512:640] * inv).astype(bf16)

    def offset(i):
        away, odd = (i + 1) // 2, i % 2
        return odd * away + (1 - odd) * (ng - away)

    def route(c):
        pick = count((slots, rows), 0) == slot_row[...]
        pick = pick.astype(f32).astype(bf16)
        moved = dot(pick, qrot[c]).astype(bf16)
        sendq[c] = moved.reshape(ng, block, 384)

        def go(i, carry):
            g = (me + offset(i)) % ng
            remote(
                sendq.at[c, g], recvq.at[c, me], q_send.at[c], q_recv.at[c, me], {"group": g}
            ).start()
            return carry

        lax.fori_loop(1, ng, go, 0)
        recvq[c, me] = sendq[c, me]

    def fresh(c):
        keys = (c + 1) * rows
        row = lax.broadcasted_iota(jnp.int32, (rows, keys), 0)
        col = lax.broadcasted_iota(jnp.int32, (rows, keys), 1)
        same = (row % part) == (col % part)
        causal = (col // part) <= (row // part + c * cs)
        ok = same & causal
        for h in range(HEADS):
            lanes = slice(h * 128, (h + 1) * 128)
            s = lax.dot_general(qrot[c, :, lanes], kn[0:keys], NT, preferred_element_type=f32)
            s = jnp.where(ok, s * SCALE, LOW)
            m = jnp.max(s, axis=1, keepdims=True)
            w = jnp.exp(s - m).astype(bf16)
            total = jnp.sum(w.astype(f32), axis=1, keepdims=True)
            o = dot(w, vn[0:keys])
            newo[c, :, lanes] = o / total
            newl[c, h] = jnp.broadcast_to(m + jnp.log(total), (rows, 128))

    many = min(4, ng)
    block3 = HEADS * block
    tall3 = many * block3
    lane3 = count((tall3, 128), 1)
    rank3 = (count((tall3, 128), 0) % block) // cs
    wide_l = recvl.shape[3]
    lane_s = count((tall3, wide_l), 1)
    row3 = count((tall3, wide_l), 0) % block3

    def cached(c, sources):
        slot = [
            [
                jnp.clip(table_s[src // two, (src % two) * cap + r], 0, part - 1)
                for r in range(cap)
            ]
            for src in sources
        ]
        scores = []
        for src, own in zip(sources, slot):
            got = recvq[c, src]
            q = jnp.concatenate([got[:, h * 128:(h + 1) * 128] for h in range(HEADS)], axis=0)
            keys = jnp.concatenate([k_v[a] for a in own], axis=0)
            s = lax.dot_general(q, keys, NT, preferred_element_type=f32) * SCALE
            best = None
            for r, a in enumerate(own):
                length = lengths_s[me * part + a]
                one = jnp.where(lane3[0:block3] < length, s[:, r * 128:(r + 1) * 128], LOW)
                best = one if best is None else jnp.where(rank3[0:block3] == r, one, best)
            scores.append(best)
        s = jnp.concatenate(scores, axis=0)
        m = jnp.max(s, axis=1, keepdims=True)
        w = jnp.exp(s - m).astype(bf16).astype(f32)
        total = jnp.sum(w, axis=1, keepdims=True)
        w = jnp.concatenate([jnp.where(rank3 == r, w, 0.0).astype(bf16) for r in range(cap)], axis=1)
        lse = jnp.where(lane_s == row3, m + jnp.log(total), 0.0)
        stats = [
            jnp.sum(lse[n * block3:(n + 1) * block3], axis=0, keepdims=True)
            for n in range(many)
        ]
        inverse = 1.0 / total
        results = []
        for n, own in enumerate(slot):
            base = n * block3
            values = jnp.concatenate([v_v[a] for a in own], axis=0)
            o = (dot(w[base:base + block3], values) * inverse[base:base + block3]).astype(bf16)
            both = [o[h * block:(h + 1) * block] for h in range(HEADS)]
            results.append(jnp.concatenate(both, axis=1))
        return results, stats

    def serve_some(c, start, skip):
        sources = [(me + 2 * ng - offset(start + n)) % ng for n in range(many)]
        for src in sources[skip:]:
            remote(
                recvq.at[c, src], recvq.at[c, src], q_send.at[c], q_recv.at[c, src],
                {"group": src},
            ).wait_recv()
        results, stats = cached(c, sources)
        if skip:
            recvo[c, me] = results[0]
            recvl[c, me] = stats[0]
        for src, result, stat in zip(sources[skip:], results[skip:], stats[skip:]):
            sendo[c, src] = result
            sendl[c, src] = stat
        for src in sources[skip:]:
            remote(
                sendo.at[c, src], recvo.at[c, me], o_send.at[c], o_recv.at[c], {"group": src}
            ).start()
            remote(
                sendl.at[c, src], recvl.at[c, me], l_send.at[c], l_recv.at[c], {"group": src}
            ).start()

    def serve_span(c, lo, hi):
        def go(i, carry):
            serve_some(c, i * many, 0)
            return carry

        if lo == 0:
            serve_some(c, 0, 1)
        lax.fori_loop(max(lo, 1), hi, go, 0)

    batches = ng // many

    def serve(c):
        serve_span(c, 0, batches)

    def serve_near(c):
        serve_span(c, 0, batches // 2)

    def serve_far(c):
        serve_span(c, batches // 2, batches)

    def combine(c):
        span = pl.ds(0, ng - 1)
        remote(
            sendo.at[c, span], recvo.at[c, span], o_send.at[c], o_recv.at[c],
            {"group": (me + 1) % ng},
        ).wait_recv()
        remote(
            sendl.at[c, span], recvl.at[c, span], l_send.at[c], l_recv.at[c],
            {"group": (me + 1) % ng},
        ).wait_recv()
        wide = jnp.concatenate([slot_col[...]] * (slots // 128), axis=1)
        pick = count((rows, slots), 1) == wide
        pick = pick.astype(f32).astype(bf16)
        back = dot(pick, recvo[c].reshape(slots, 384))
        stat = recvl[c].reshape(ng, wide_l)
        hi = stat.astype(bf16)
        mid = (stat - hi.astype(f32)).astype(bf16)
        lo = (stat - hi.astype(f32) - mid.astype(f32)).astype(bf16)
        home = slot_col[:, 0:ng] // block
        home = (count((rows, ng), 1) == home).astype(f32).astype(bf16)
        terms = dot(home, jnp.concatenate([hi, mid, lo], axis=1))
        stat = terms[:, 0:wide_l] + terms[:, wide_l:2 * wide_l] + terms[:, 2 * wide_l:]
        spot = count((rows, wide_l), 1) - slot_col[:, 0:1] % block
        for h in range(HEADS):
            lanes = slice(h * 128, (h + 1) * 128)
            cache_l = jnp.sum(jnp.where(spot == h * block, stat, 0.0), axis=1, keepdims=True)
            gap = newl[c, h] - cache_l
            a = 1.0 / (1.0 + jnp.exp(gap))
            b = 1.0 / (1.0 + jnp.exp(-gap))
            att[:, lanes] = (back[:, lanes] * a + newo[c, :, lanes] * b).astype(bf16)

    order = (xf, xr, xl, x)

    def give(c):
        for n, xi in enumerate(order):
            other[c, n] = dot(att[...], wo_v[shard_of(xi, 1 - core)]).astype(bf16)
            send(other.at[c, n], fromp.at[c, n], p_send.at[c, n], p_recv.at[c, n], partner)
        for n, xi in enumerate(order):
            mine[c, n] = dot(att[...], wo_v[shard_of(xi, core)]).astype(bf16)

    top, low = slice(0, half), slice(half, rows)

    def chip_sum(c, n, at):
        return mine[c, n, at].astype(f32) + fromp[c, n, at].astype(f32)

    def spread(c):
        arrived(fromp.at[c, 0], p_recv.at[c, 0])
        far[c] = chip_sum(c, 0, slice(0, rows)).astype(bf16)
        send(far.at[c, pl.ds(0, half)], ring_far.at[c, 0], far_send.at[c, 0], far_recv.at[c, 0], right)
        send(far.at[c, pl.ds(half, half)], ring_far.at[c, 1], far_send.at[c, 1], far_recv.at[c, 1], left)
        arrived(fromp.at[c, 1], p_recv.at[c, 1])
        side[c, 0, 1] = chip_sum(c, 1, low).astype(bf16)
        send(side.at[c, 0, 1], ring_side.at[c, 0, 1], side_send.at[c, 0, 1], side_recv.at[c, 0, 1], right)
        arrived(fromp.at[c, 2], p_recv.at[c, 2])
        side[c, 1, 0] = chip_sum(c, 2, top).astype(bf16)
        send(side.at[c, 1, 0], ring_side.at[c, 1, 0], side_send.at[c, 1, 0], side_recv.at[c, 1, 0], left)

    def relay(c):
        arrived(ring_far.at[c, 0], far_recv.at[c, 0])
        side[c, 0, 0] = (chip_sum(c, 1, top) + ring_far[c, 0].astype(f32)).astype(bf16)
        send(side.at[c, 0, 0], ring_side.at[c, 0, 0], side_send.at[c, 0, 0], side_recv.at[c, 0, 0], right)
        arrived(ring_far.at[c, 1], far_recv.at[c, 1])
        side[c, 1, 1] = (chip_sum(c, 2, low) + ring_far[c, 1].astype(f32)).astype(bf16)
        send(side.at[c, 1, 1], ring_side.at[c, 1, 1], side_send.at[c, 1, 1], side_recv.at[c, 1, 1], left)

    outs = []

    def finish(c):
        arrived(fromp.at[c, 3], p_recv.at[c, 3])
        for n in (1, 0):
            for s in (1, 0) if n == 0 else (0, 1):
                arrived(ring_side.at[c, s, n], side_recv.at[c, s, n])
            at = slice(n * half, (n + 1) * half)
            total = chip_sum(c, 3, at)
            total = total + ring_side[c, 0, n].astype(f32) + ring_side[c, 1, n].astype(f32)
            outv[c * cs + n * hs:c * cs + (n + 1) * hs] = total.astype(bf16).reshape(hs, part, feat)
        copy = pltpu.make_async_copy(
            outv.at[pl.ds(c * cs, cs)], out_hbm.at[pl.ds(c * cs, cs)], out_sem.at[c]
        )
        copy.start()
        outs.append(copy)

    phases = {
        "s": serve_near, "t": serve_far,
        "A": project, "B": project_rest, "R": route, "F": fresh, "S": serve,
        "C": combine, "V": give, "P": spread, "L": relay, "N": finish,
    }
    done = ""
    for step in ORDER:
        if step[0] in "Ss" and not set("Ss") & set(done):
            for copy in copies + [table_copy]:
                copy.wait()
        if step[0] == "V" and "V" not in done:
            for copy in wo_copies:
                copy.wait()
        phases[step[0]](int(step[1]))
        done += step[0]

    for copy in pending:
        copy.wait_send()
    span = pl.ds(0, ng - 1)
    for c in range(chunks):
        remote(
            sendq.at[c, span], recvq.at[c, span], q_send.at[c], q_recv.at[c, 0],
            {"group": (me + 1) % ng},
        ).wait_send()
        remote(
            sendo.at[c, span], recvo.at[c, span], o_send.at[c], o_recv.at[c],
            {"group": (me + 1) % ng},
        ).wait_send()
        remote(
            sendl.at[c, span], recvl.at[c, span], l_send.at[c], l_recv.at[c],
            {"group": (me + 1) % ng},
        ).wait_send()
    for copy in outs:
        copy.wait()


def call(dims, *args):
    ng, nt, steps, part, feat, cap, chunks = dims
    cs = steps // chunks
    rows = cs * part
    block = cap * cs
    wide_l = -(-HEADS * block // 128) * 128
    any_ = pl.BlockSpec(memory_space=pl.ANY)
    vmem = pl.BlockSpec(memory_space=pltpu.VMEM)
    smem = pl.BlockSpec(memory_space=pltpu.SMEM)
    dma = pltpu.SemaphoreType.DMA
    V = pltpu.VMEM
    scratch = [
        V((nt, steps, part, feat), bf16), V((nt, feat, 640), bf16), V((nt, 384, feat), bf16),
        V((part, 128, 128), bf16), V((part, 128, 128), bf16),
        V((steps * part, 128), f32), V((steps * part, 128), f32),
        V((1, rows), jnp.int32), V((rows, 128), jnp.int32),
        V((ng * part // 128, 128), jnp.int32),
        pltpu.SMEM((ng * part // 128, 128), jnp.int32),
        V((rows, 640), f32), V((rows, 128), f32), V((chunks, rows, 384), bf16),
        V((steps * part, 128), bf16), V((steps * part, 128), bf16),
        V((chunks, rows, 384), f32), V((chunks, HEADS, rows, 128), f32),
        V((chunks, ng, block, 384), bf16), V((chunks, ng, block, 384), bf16),
        V((chunks, ng, block, 384), bf16), V((chunks, ng, block, 384), bf16),
        V((chunks, ng, 1, wide_l), f32), V((chunks, ng, 1, wide_l), f32),
        V((rows, 384), bf16),
        V((chunks, 4, rows, feat), bf16), V((chunks, 4, rows, feat), bf16),
        V((chunks, 4, rows, feat), bf16),
        V((chunks, rows, feat), bf16), V((chunks, 2, rows // 2, feat), bf16),
        V((chunks, 2, 2, rows // 2, feat), bf16), V((chunks, 2, 2, rows // 2, feat), bf16),
        V((steps, part, feat), bf16),
        dma((4 + 4 * nt,)), dma((chunks, 9)), dma((chunks, 9)),
        dma((chunks,)), dma((chunks, ng)), dma((chunks,)), dma((chunks,)),
        dma((chunks,)), dma((chunks,)),
        dma((chunks, 4)), dma((chunks, 4)), dma((chunks, 2)), dma((chunks, 2)),
        dma((chunks, 2, 2)), dma((chunks, 2, 2)), dma((chunks,)),
    ]
    return pl.pallas_call(
        functools.partial(kernel, dims),
        out_shape=jax.ShapeDtypeStruct((steps, part, feat), bf16),
        in_specs=[any_, vmem] + [any_] * 6 + [vmem, vmem, vmem, smem, vmem],
        out_specs=any_,
        scratch_shapes=scratch,
        compiler_params=pltpu.CompilerParams(
            collective_id=0, has_side_effects=True, vmem_limit_bytes=62 * 1024 * 1024
        ),
    )(*args)


def local(
    states, norm_gain, w_query, w_key, w_value, w_out, key_cache, value_cache,
    ancestor_group, ancestor_slot, lengths,
):
    part, steps, feat = states.shape
    ng, nt = lax.axis_size("group"), lax.axis_size("tensor")
    cap = max(2, (2 * part + ng - 1) // ng)
    dims = (ng, nt, steps, part, feat, cap, CHUNKS)
    index = np.arange(64, dtype=np.float64)
    inverse = np.float64(THETA) ** (-2.0 * index / 128)
    wide = np.concatenate([inverse, inverse])
    angles = np.arange(steps)[:, None] * wide[None, :]
    turns = np.zeros((8 + 2 * steps, 128))
    turns[0] = wide
    turns[1] = np.where(np.arange(128) < 64, -1.0, 1.0)
    turns[8:8 + steps] = np.cos(angles)
    turns[8 + steps:] = np.sin(angles)
    out = call(
        dims,
        jnp.transpose(states, (1, 0, 2)),
        norm_gain.reshape(-1, 128),
        w_query, w_key, w_value, w_out, key_cache, value_cache,
        ancestor_group.reshape(-1, 128), ancestor_slot.reshape(-1, 128),
        lengths.reshape(-1, 128), lengths, jnp.asarray(turns, f32),
    )
    return jnp.transpose(out, (1, 0, 2))


def solution(mesh):
    in_specs = (
        P("group", None, "tensor"),
        P(),
        P(None, "tensor"),
        P(None, "tensor"),
        P(None, "tensor"),
        P("tensor", None),
        P("group", None, "tensor"),
        P("group", None, "tensor"),
        P(),
        P(),
        P(),
    )
    out_specs = P("group", None, "tensor")
    return jax.shard_map(local, mesh=mesh, in_specs=in_specs, out_specs=out_specs, check_vma=False)
```

```python
import functools
import math

import jax
import jax.numpy as jnp
import numpy as np
from jax import lax
from jax.experimental import pallas as pl
from jax.experimental.pallas import tpu as pltpu
from jax.sharding import PartitionSpec as P

MESH = pl.DeviceIdType.MESH
HEAD = 128
HEADS = 3
CHUNKS = 3
ORDER = (
    "A0", "B0", "R0", "A1", "s0", "B1", "R1", "t0", "F0", "A2",
    "s1", "B2", "R2", "t1", "F1", "C0", "V0", "P0", "s2", "L0",
    "t2", "F2", "C1", "V1", "P1", "N0", "L1", "C2", "V2", "P2",
    "N1", "L2", "N2",
)
THETA = 1000000.0
EPS = 1e-06
LOW = -1e30
SCALE = 1.0 / math.sqrt(HEAD)
NT = (((1,), (1,)), ((), ()))
f32 = jnp.float32
bf16 = jnp.bfloat16


def dot(a, b):
    return jnp.dot(a, b, preferred_element_type=f32)


def kernel(
    dims,
    x_hbm, gain_ref, wq_hbm, wk_hbm, wv_hbm, wo_hbm, kc_hbm, vc_hbm,
    group_ref, place_ref, length_ref, lengths_s, turns_ref,
    out_hbm,
    xg, w_v, wo_v, k_v, v_v, cos_v, sin_v, slot_row, slot_col, table_v, table_s,
    acc, ssq, qrot, kn, vn, newo, newl,
    sendq, recvq, sendo, recvo, sendl, recvl, att,
    mine, other, fromp, far, ring_far, side, ring_side, outv,
    local_sem, ag_send, ag_recv, q_send, q_recv, o_send, o_recv, l_send, l_recv,
    p_send, p_recv, far_send, far_recv, side_send, side_recv, out_sem,
):
    ng, nt, steps, part, feat, cap, chunks = dims
    cs = steps // chunks
    rows = cs * part
    half = rows // 2
    hs = cs // 2
    block = cap * cs
    slots = ng * block
    blocks = feat // 128
    nx = nt // 2

    me = lax.axis_index("group")
    t = lax.axis_index("tensor")
    x, core = t // 2, t % 2
    xr, xl, xf = (x + 1) % nx, (x + nx - 1) % nx, (x + 2) % nx
    right, left, partner = xr * 2 + core, xl * 2 + core, x * 2 + 1 - core
    pending = []

    def remote(src, dst, ssem, rsem, dev):
        return pltpu.make_async_remote_copy(
            src_ref=src, dst_ref=dst, send_sem=ssem, recv_sem=rsem,
            device_id=dev, device_id_type=MESH,
        )

    def send(src, dst, ssem, rsem, dev):
        copy = remote(src, dst, ssem, rsem, {"tensor": dev})
        copy.start()
        pending.append(copy)

    def arrived(dst, rsem):
        remote(dst, dst, rsem, rsem, {"tensor": partner}).wait_recv()

    first = pltpu.make_async_copy(x_hbm, xg.at[t], local_sem.at[0])
    first.start()

    barrier = pltpu.get_barrier_semaphore()
    for dev in (right, left, partner):
        pl.semaphore_signal(barrier, inc=1, device_id={"tensor": dev}, device_id_type=MESH)

    def greet(i, carry):
        pl.semaphore_signal(
            barrier, inc=1, device_id={"group": (me + i) % ng}, device_id_type=MESH
        )
        return carry

    lax.fori_loop(1, ng, greet, 0)

    copies = [
        pltpu.make_async_copy(kc_hbm, k_v, local_sem.at[1]),
        pltpu.make_async_copy(vc_hbm, v_v, local_sem.at[2]),
    ]
    sem = 3
    w_copies, wo_copies = [], []
    for j in range(nt):
        lo = j * feat
        for ref, at, wide in ((wq_hbm, 0, 384), (wk_hbm, 384, 128), (wv_hbm, 512, 128)):
            w_copies.append(
                pltpu.make_async_copy(
                    ref.at[pl.ds(lo, feat)],
                    w_v.at[j, :, pl.ds(at, wide)],
                    local_sem.at[sem],
                )
            )
            sem += 1
    for j in range(nt):
        wo_copies.append(
            pltpu.make_async_copy(
                wo_hbm.at[:, pl.ds(j * feat, feat)], wo_v.at[j], local_sem.at[sem]
            )
        )
        sem += 1
    first.wait()
    pl.semaphore_wait(barrier, 3 + ng - 1)

    def piece(shard, c, lo=0, count=cs):
        return xg.at[shard, pl.ds(c * cs + lo, count)]

    def ag_start(c):
        own = piece(t, c)
        send(own, own, ag_send.at[c, 0], ag_recv.at[c, 0], right)
        send(own, own, ag_send.at[c, 1], ag_recv.at[c, 1], left)
        send(own, own, ag_send.at[c, 2], ag_recv.at[c, 2], partner)

    ag_start(0)
    for copy in w_copies:
        copy.start()
    for copy in w_copies:
        copy.wait()

    def fold(b, carry):
        j, i = b // blocks, b % blocks
        lane = jnp.broadcast_to(gain_ref[pl.ds(b, 1), :], (128, 128))
        tall = jnp.transpose(lane)
        at = pl.ds(pl.multiple_of(i * 128, 128), 128)
        for n in range(5):
            cols = slice(n * 128, (n + 1) * 128)
            w_v[j, at, cols] = (w_v[j, at, cols].astype(f32) * tall).astype(bf16)
        return carry

    lax.fori_loop(0, nt * blocks, fold, 0)

    def count(shape, axis):
        return lax.broadcasted_iota(jnp.int32, shape, axis)

    two = 128 // part
    lines = ng // two
    row_i, col_i = count((128, 128), 0), count((128, 128), 1)
    lane_l = count((lines, 128), 1)
    asked = jnp.where(group_ref[...] == me, 1, 0)
    within = lane_l % part
    rank = asked
    hop = 1
    while hop < part:
        rank = rank + jnp.where(within >= hop, pltpu.roll(rank, hop, 1), 0)
        hop *= 2
    table = jnp.zeros((lines, 128), jnp.int32)
    for r in range(cap):
        found = jnp.where((asked == 1) & (rank == r + 1), place_ref[...], 0)
        hop = 1
        while hop < part:
            found = found + jnp.where(within >= hop, pltpu.roll(found, hop, 1), 0)
            hop *= 2
        for n in range(two):
            to = n * cap + r
            moved = pltpu.roll(found, (to - (n + 1) * part + 1) % 128, 1)
            table = jnp.where(lane_l == to, moved, table)
    table_v[...] = table
    table_copy = pltpu.make_async_copy(table_v, table_s, local_sem.at[3 + 4 * nt])
    table_copy.start()

    def own_line(ref):
        line = ref[pl.ds(me // two, 1), :].astype(f32)
        best = line
        for n in range(1, two):
            best = jnp.where(me % two == n, pltpu.roll(line, 128 - n * part, 1), best)
        return best

    wide_group = jnp.broadcast_to(own_line(group_ref), (128, 128))
    wide_place = jnp.broadcast_to(own_line(place_ref), (128, 128))
    tall_group, tall_place = jnp.transpose(wide_group), jnp.transpose(wide_place)
    match = (wide_group == tall_group).astype(f32)
    row_rank = jnp.sum(jnp.where(row_i < col_i, match, 0.0), axis=0, keepdims=True)
    col_rank = jnp.sum(jnp.where(col_i < row_i, match, 0.0), axis=1, keepdims=True)
    row_slot = (wide_group[0:1] * cap + row_rank) * cs
    col_slot = (tall_group * cap + col_rank) * cs
    row_slot = jnp.where(count((1, 128), 1) < part, row_slot, 0.0)
    for n in range(1, two):
        row_slot = row_slot + jnp.where(
            count((1, 128), 1) // part == n, pltpu.roll(row_slot, n * part, 1), 0.0
        )
    for n in range(cs // two):
        ahead = row_slot + (count((1, 128), 1) // part + n * two).astype(f32)
        slot_row[:, n * 128:(n + 1) * 128] = ahead.astype(jnp.int32)
    for n in range(cs):
        slot_col[n * part:(n + 1) * part] = (col_slot[0:part] + n).astype(jnp.int32)
    which = (tall_group * (1.0 / two)).astype(jnp.int32)
    rest = tall_group.astype(jnp.int32) - which * two
    line_of = (which[0:part, 0:lines] == count((part, lines), 1)).astype(f32).astype(bf16)
    near = dot(line_of, length_ref[...].astype(f32).astype(bf16))
    at_lane = rest * part + tall_place.astype(jnp.int32)
    near = jnp.where(count((part, 128), 1) == at_lane[0:part], near, 0.0)
    span_col = jnp.sum(near, axis=1, keepdims=True)
    angle = span_col * turns_ref[0:1]
    cos_a, sin_a = jnp.cos(angle), jnp.sin(angle)
    for n in range(steps):
        cos_b, sin_b = turns_ref[8 + n:9 + n], turns_ref[8 + steps + n:9 + steps + n]
        cos_v[n * part:(n + 1) * part] = cos_a * cos_b - sin_a * sin_b
        sin_v[n * part:(n + 1) * part] = (sin_a * cos_b + cos_a * sin_b) * turns_ref[1:2]

    def shard_dot(shard, c, first=False):
        xs = xg[shard, c * cs:(c + 1) * cs].reshape(rows, feat)
        product = dot(xs, w_v[shard])
        wide = xs.astype(f32)
        squares = wide[:, 0:128] * wide[:, 0:128]
        for i in range(1, blocks):
            part_ = wide[:, i * 128:(i + 1) * 128]
            squares = squares + part_ * part_
        if first:
            acc[...] = product
            ssq[...] = squares
        else:
            acc[...] += product
            ssq[...] += squares

    def shard_of(xi, co):
        return xi * 2 + co

    sl, sr, sf = shard_of(xl, core), shard_of(xr, core), shard_of(xf, core)

    def project(c):
        arrived(piece(sl, c), ag_recv.at[c, 0])
        send(piece(sl, c, 0, hs), piece(sl, c, 0, hs), ag_send.at[c, 3], ag_recv.at[c, 3], right)
        send(piece(sl, c), piece(sl, c), ag_send.at[c, 4], ag_recv.at[c, 4], partner)
        arrived(piece(sr, c), ag_recv.at[c, 1])
        send(piece(sr, c, hs, hs), piece(sr, c, hs, hs), ag_send.at[c, 5], ag_recv.at[c, 5], left)
        send(piece(sr, c), piece(sr, c), ag_send.at[c, 6], ag_recv.at[c, 6], partner)
        if c + 1 < chunks:
            ag_start(c + 1)
        shard_dot(t, c, True)
        arrived(piece(partner, c), ag_recv.at[c, 2])
        shard_dot(partner, c)
        shard_dot(sl, c)
        shard_dot(sr, c)

    def project_rest(c):
        if c == 0:
            for copy in copies + wo_copies:
                copy.start()
        arrived(piece(sf, c, 0, hs), ag_recv.at[c, 3])
        send(piece(sf, c, 0, hs), piece(sf, c, 0, hs), ag_send.at[c, 7], ag_recv.at[c, 7], partner)
        arrived(piece(sf, c, hs, hs), ag_recv.at[c, 5])
        send(piece(sf, c, hs, hs), piece(sf, c, hs, hs), ag_send.at[c, 8], ag_recv.at[c, 8], partner)
        shard_dot(sf, c)
        pl_, pr, pf = shard_of(xl, 1 - core), shard_of(xr, 1 - core), shard_of(xf, 1 - core)
        arrived(piece(pl_, c), ag_recv.at[c, 4])
        shard_dot(pl_, c)
        arrived(piece(pr, c), ag_recv.at[c, 6])
        shard_dot(pr, c)
        arrived(piece(pf, c, 0, hs), ag_recv.at[c, 7])
        arrived(piece(pf, c, hs, hs), ag_recv.at[c, 8])
        shard_dot(pf, c)
        mean = jnp.sum(ssq[...], axis=1, keepdims=True) * (1.0 / (nt * feat))
        inv = lax.rsqrt(mean + EPS)
        here = slice(c * rows, (c + 1) * rows)
        cos, sin = cos_v[here], sin_v[here]

        def turn(v):
            v = v * inv
            return (v * cos + pltpu.roll(v, 64, 1) * sin).astype(bf16)

        for h in range(HEADS):
            qrot[c, :, h * 128:(h + 1) * 128] = turn(acc[:, h * 128:(h + 1) * 128])
        kn[here] = turn(acc[:, 384:512])
        vn[here] = (acc[:, 512:640] * inv).astype(bf16)

    def offset(i):
        away, odd = (i + 1) // 2, i % 2
        return odd * away + (1 - odd) * (ng - away)

    def route(c):
        pick = count((slots, rows), 0) == slot_row[...]
        pick = pick.astype(f32).astype(bf16)
        moved = dot(pick, qrot[c]).astype(bf16)
        sendq[c] = moved.reshape(ng, block, 384)

        def go(i, carry):
            g = (me + offset(i)) % ng
            remote(
                sendq.at[c, g], recvq.at[c, me], q_send.at[c], q_recv.at[c, me], {"group": g}
            ).start()
            return carry

        lax.fori_loop(1, ng, go, 0)
        recvq[c, me] = sendq[c, me]

    def fresh(c):
        keys = (c + 1) * rows
        row = lax.broadcasted_iota(jnp.int32, (rows, keys), 0)
        col = lax.broadcasted_iota(jnp.int32, (rows, keys), 1)
        same = (row % part) == (col % part)
        causal = (col // part) <= (row // part + c * cs)
        ok = same & causal
        for h in range(HEADS):
            lanes = slice(h * 128, (h + 1) * 128)
            s = lax.dot_general(qrot[c, :, lanes], kn[0:keys], NT, preferred_element_type=f32)
            s = jnp.where(ok, s * SCALE, LOW)
            m = jnp.max(s, axis=1, keepdims=True)
            w = jnp.exp(s - m).astype(bf16)
            total = jnp.sum(w.astype(f32), axis=1, keepdims=True)
            o = dot(w, vn[0:keys])
            newo[c, :, lanes] = o / total
            newl[c, h] = jnp.broadcast_to(m + jnp.log(total), (rows, 128))

    many = min(4, ng)
    block3 = HEADS * block
    tall3 = many * block3
    lane3 = count((tall3, 128), 1)
    rank3 = (count((tall3, 128), 0) % block) // cs
    wide_l = recvl.shape[3]
    lane_s = count((tall3, wide_l), 1)
    row3 = count((tall3, wide_l), 0) % block3

    def cached(c, sources):
        slot = [
            [
                jnp.clip(table_s[src // two, (src % two) * cap + r], 0, part - 1)
                for r in range(cap)
            ]
            for src in sources
        ]
        scores = []
        for src, own in zip(sources, slot):
            got = recvq[c, src]
            q = jnp.concatenate([got[:, h * 128:(h + 1) * 128] for h in range(HEADS)], axis=0)
            keys = jnp.concatenate([k_v[a] for a in own], axis=0)
            s = lax.dot_general(q, keys, NT, preferred_element_type=f32) * SCALE
            best = None
            for r, a in enumerate(own):
                length = lengths_s[me * part + a]
                one = jnp.where(lane3[0:block3] < length, s[:, r * 128:(r + 1) * 128], LOW)
                best = one if best is None else jnp.where(rank3[0:block3] == r, one, best)
            scores.append(best)
        s = jnp.concatenate(scores, axis=0)
        m = jnp.max(s, axis=1, keepdims=True)
        w = jnp.exp(s - m).astype(bf16).astype(f32)
        total = jnp.sum(w, axis=1, keepdims=True)
        w = jnp.concatenate([jnp.where(rank3 == r, w, 0.0).astype(bf16) for r in range(cap)], axis=1)
        lse = jnp.where(lane_s == row3, m + jnp.log(total), 0.0)
        stats = [
            jnp.sum(lse[n * block3:(n + 1) * block3], axis=0, keepdims=True)
            for n in range(many)
        ]
        inverse = 1.0 / total
        results = []
        for n, own in enumerate(slot):
            base = n * block3
            values = jnp.concatenate([v_v[a] for a in own], axis=0)
            o = (dot(w[base:base + block3], values) * inverse[base:base + block3]).astype(bf16)
            both = [o[h * block:(h + 1) * block] for h in range(HEADS)]
            results.append(jnp.concatenate(both, axis=1))
        return results, stats

    def serve_some(c, start, skip):
        sources = [(me + 2 * ng - offset(start + n)) % ng for n in range(many)]
        for src in sources[skip:]:
            remote(
                recvq.at[c, src], recvq.at[c, src], q_send.at[c], q_recv.at[c, src],
                {"group": src},
            ).wait_recv()
        results, stats = cached(c, sources)
        if skip:
            recvo[c, me] = results[0]
            recvl[c, me] = stats[0]
        for src, result, stat in zip(sources[skip:], results[skip:], stats[skip:]):
            sendo[c, src] = result
            sendl[c, src] = stat
        for src in sources[skip:]:
            remote(
                sendo.at[c, src], recvo.at[c, me], o_send.at[c], o_recv.at[c], {"group": src}
            ).start()
            remote(
                sendl.at[c, src], recvl.at[c, me], l_send.at[c], l_recv.at[c], {"group": src}
            ).start()

    def serve_span(c, lo, hi):
        def go(i, carry):
            serve_some(c, i * many, 0)
            return carry

        if lo == 0:
            serve_some(c, 0, 1)
        lax.fori_loop(max(lo, 1), hi, go, 0)

    batches = ng // many

    def serve(c):
        serve_span(c, 0, batches)

    def serve_near(c):
        serve_span(c, 0, batches // 2)

    def serve_far(c):
        serve_span(c, batches // 2, batches)

    def combine(c):
        span = pl.ds(0, ng - 1)
        remote(
            sendo.at[c, span], recvo.at[c, span], o_send.at[c], o_recv.at[c],
            {"group": (me + 1) % ng},
        ).wait_recv()
        remote(
            sendl.at[c, span], recvl.at[c, span], l_send.at[c], l_recv.at[c],
            {"group": (me + 1) % ng},
        ).wait_recv()
        wide = jnp.concatenate([slot_col[...]] * (slots // 128), axis=1)
        pick = count((rows, slots), 1) == wide
        pick = pick.astype(f32).astype(bf16)
        back = dot(pick, recvo[c].reshape(slots, 384))
        stat = recvl[c].reshape(ng, wide_l)
        hi = stat.astype(bf16)
        mid = (stat - hi.astype(f32)).astype(bf16)
        lo = (stat - hi.astype(f32) - mid.astype(f32)).astype(bf16)
        home = slot_col[:, 0:ng] // block
        home = (count((rows, ng), 1) == home).astype(f32).astype(bf16)
        terms = dot(home, jnp.concatenate([hi, mid, lo], axis=1))
        stat = terms[:, 0:wide_l] + terms[:, wide_l:2 * wide_l] + terms[:, 2 * wide_l:]
        spot = count((rows, wide_l), 1) - slot_col[:, 0:1] % block
        for h in range(HEADS):
            lanes = slice(h * 128, (h + 1) * 128)
            cache_l = jnp.sum(jnp.where(spot == h * block, stat, 0.0), axis=1, keepdims=True)
            gap = newl[c, h] - cache_l
            a = 1.0 / (1.0 + jnp.exp(gap))
            b = 1.0 / (1.0 + jnp.exp(-gap))
            att[:, lanes] = (back[:, lanes] * a + newo[c, :, lanes] * b).astype(bf16)

    order = (xf, xr, xl, x)

    def give(c):
        for n, xi in enumerate(order):
            other[c, n] = dot(att[...], wo_v[shard_of(xi, 1 - core)]).astype(bf16)
            send(other.at[c, n], fromp.at[c, n], p_send.at[c, n], p_recv.at[c, n], partner)
        for n, xi in enumerate(order):
            mine[c, n] = dot(att[...], wo_v[shard_of(xi, core)]).astype(bf16)

    top, low = slice(0, half), slice(half, rows)

    def chip_sum(c, n, at):
        return mine[c, n, at].astype(f32) + fromp[c, n, at].astype(f32)

    def spread(c):
        arrived(fromp.at[c, 0], p_recv.at[c, 0])
        far[c] = chip_sum(c, 0, slice(0, rows)).astype(bf16)
        send(far.at[c, pl.ds(0, half)], ring_far.at[c, 0], far_send.at[c, 0], far_recv.at[c, 0], right)
        send(far.at[c, pl.ds(half, half)], ring_far.at[c, 1], far_send.at[c, 1], far_recv.at[c, 1], left)
        arrived(fromp.at[c, 1], p_recv.at[c, 1])
        side[c, 0, 1] = chip_sum(c, 1, low).astype(bf16)
        send(side.at[c, 0, 1], ring_side.at[c, 0, 1], side_send.at[c, 0, 1], side_recv.at[c, 0, 1], right)
        arrived(fromp.at[c, 2], p_recv.at[c, 2])
        side[c, 1, 0] = chip_sum(c, 2, top).astype(bf16)
        send(side.at[c, 1, 0], ring_side.at[c, 1, 0], side_send.at[c, 1, 0], side_recv.at[c, 1, 0], left)

    def relay(c):
        arrived(ring_far.at[c, 0], far_recv.at[c, 0])
        side[c, 0, 0] = (chip_sum(c, 1, top) + ring_far[c, 0].astype(f32)).astype(bf16)
        send(side.at[c, 0, 0], ring_side.at[c, 0, 0], side_send.at[c, 0, 0], side_recv.at[c, 0, 0], right)
        arrived(ring_far.at[c, 1], far_recv.at[c, 1])
        side[c, 1, 1] = (chip_sum(c, 2, low) + ring_far[c, 1].astype(f32)).astype(bf16)
        send(side.at[c, 1, 1], ring_side.at[c, 1, 1], side_send.at[c, 1, 1], side_recv.at[c, 1, 1], left)

    outs = []

    def finish(c):
        arrived(fromp.at[c, 3], p_recv.at[c, 3])
        for n in (1, 0):
            for s in (1, 0) if n == 0 else (0, 1):
                arrived(ring_side.at[c, s, n], side_recv.at[c, s, n])
            at = slice(n * half, (n + 1) * half)
            total = chip_sum(c, 3, at)
            total = total + ring_side[c, 0, n].astype(f32) + ring_side[c, 1, n].astype(f32)
            outv[c * cs + n * hs:c * cs + (n + 1) * hs] = total.astype(bf16).reshape(hs, part, feat)
        copy = pltpu.make_async_copy(
            outv.at[pl.ds(c * cs, cs)], out_hbm.at[pl.ds(c * cs, cs)], out_sem.at[c]
        )
        copy.start()
        outs.append(copy)

    phases = {
        "s": serve_near, "t": serve_far,
        "A": project, "B": project_rest, "R": route, "F": fresh, "S": serve,
        "C": combine, "V": give, "P": spread, "L": relay, "N": finish,
    }
    done = ""
    for step in ORDER:
        if step[0] in "Ss" and not set("Ss") & set(done):
            for copy in copies + [table_copy]:
                copy.wait()
        if step[0] == "V" and "V" not in done:
            for copy in wo_copies:
                copy.wait()
        phases[step[0]](int(step[1]))
        done += step[0]

    for copy in pending:
        copy.wait_send()
    span = pl.ds(0, ng - 1)
    for c in range(chunks):
        remote(
            sendq.at[c, span], recvq.at[c, span], q_send.at[c], q_recv.at[c, 0],
            {"group": (me + 1) % ng},
        ).wait_send()
        remote(
            sendo.at[c, span], recvo.at[c, span], o_send.at[c], o_recv.at[c],
            {"group": (me + 1) % ng},
        ).wait_send()
        remote(
            sendl.at[c, span], recvl.at[c, span], l_send.at[c], l_recv.at[c],
            {"group": (me + 1) % ng},
        ).wait_send()
    for copy in outs:
        copy.wait()


def call(dims, *args):
    ng, nt, steps, part, feat, cap, chunks = dims
    cs = steps // chunks
    rows = cs * part
    block = cap * cs
    wide_l = -(-HEADS * block // 128) * 128
    any_ = pl.BlockSpec(memory_space=pl.ANY)
    vmem = pl.BlockSpec(memory_space=pltpu.VMEM)
    smem = pl.BlockSpec(memory_space=pltpu.SMEM)
    dma = pltpu.SemaphoreType.DMA
    V = pltpu.VMEM
    scratch = [
        V((nt, steps, part, feat), bf16), V((nt, feat, 640), bf16), V((nt, 384, feat), bf16),
        V((part, 128, 128), bf16), V((part, 128, 128), bf16),
        V((steps * part, 128), f32), V((steps * part, 128), f32),
        V((1, rows), jnp.int32), V((rows, 128), jnp.int32),
        V((ng * part // 128, 128), jnp.int32),
        pltpu.SMEM((ng * part // 128, 128), jnp.int32),
        V((rows, 640), f32), V((rows, 128), f32), V((chunks, rows, 384), bf16),
        V((steps * part, 128), bf16), V((steps * part, 128), bf16),
        V((chunks, rows, 384), f32), V((chunks, HEADS, rows, 128), f32),
        V((chunks, ng, block, 384), bf16), V((chunks, ng, block, 384), bf16),
        V((chunks, ng, block, 384), bf16), V((chunks, ng, block, 384), bf16),
        V((chunks, ng, 1, wide_l), f32), V((chunks, ng, 1, wide_l), f32),
        V((rows, 384), bf16),
        V((chunks, 4, rows, feat), bf16), V((chunks, 4, rows, feat), bf16),
        V((chunks, 4, rows, feat), bf16),
        V((chunks, rows, feat), bf16), V((chunks, 2, rows // 2, feat), bf16),
        V((chunks, 2, 2, rows // 2, feat), bf16), V((chunks, 2, 2, rows // 2, feat), bf16),
        V((steps, part, feat), bf16),
        dma((4 + 4 * nt,)), dma((chunks, 9)), dma((chunks, 9)),
        dma((chunks,)), dma((chunks, ng)), dma((chunks,)), dma((chunks,)),
        dma((chunks,)), dma((chunks,)),
        dma((chunks, 4)), dma((chunks, 4)), dma((chunks, 2)), dma((chunks, 2)),
        dma((chunks, 2, 2)), dma((chunks, 2, 2)), dma((chunks,)),
    ]
    return pl.pallas_call(
        functools.partial(kernel, dims),
        out_shape=jax.ShapeDtypeStruct((steps, part, feat), bf16),
        in_specs=[any_, vmem] + [any_] * 6 + [vmem, vmem, vmem, smem, vmem],
        out_specs=any_,
        scratch_shapes=scratch,
        compiler_params=pltpu.CompilerParams(
            collective_id=0, has_side_effects=True, vmem_limit_bytes=62 * 1024 * 1024
        ),
    )(*args)


def local(
    states, norm_gain, w_query, w_key, w_value, w_out, key_cache, value_cache,
    ancestor_group, ancestor_slot, lengths,
):
    part, steps, feat = states.shape
    ng, nt = lax.axis_size("group"), lax.axis_size("tensor")
    cap = max(2, (2 * part + ng - 1) // ng)
    dims = (ng, nt, steps, part, feat, cap, CHUNKS)
    index = np.arange(64, dtype=np.float64)
    inverse = np.float64(THETA) ** (-2.0 * index / 128)
    wide = np.concatenate([inverse, inverse])
    angles = np.arange(steps)[:, None] * wide[None, :]
    turns = np.zeros((8 + 2 * steps, 128))
    turns[0] = wide
    turns[1] = np.where(np.arange(128) < 64, -1.0, 1.0)
    turns[8:8 + steps] = np.cos(angles)
    turns[8 + steps:] = np.sin(angles)
    out = call(
        dims,
        jnp.transpose(states, (1, 0, 2)),
        norm_gain.reshape(-1, 128),
        w_query, w_key, w_value, w_out, key_cache, value_cache,
        ancestor_group.reshape(-1, 128), ancestor_slot.reshape(-1, 128),
        lengths.reshape(-1, 128), lengths, jnp.asarray(turns, f32),
    )
    return jnp.transpose(out, (1, 0, 2))


def solution(mesh):
    in_specs = (
        P("group", None, "tensor"),
        P(),
        P(None, "tensor"),
        P(None, "tensor"),
        P(None, "tensor"),
        P("tensor", None),
        P("group", None, "tensor"),
        P("group", None, "tensor"),
        P(),
        P(),
        P(),
    )
    out_specs = P("group", None, "tensor")
    return jax.shard_map(local, mesh=mesh, in_specs=in_specs, out_specs=out_specs, check_vma=False)
```
